32 devices in a mesh: px: 8 (over y, x, core), py: 4 (over z).
Axes of the slice: x: 2, y: 2, z: 4, core: 2. Of those that a mesh axis runs over, the one named last changes fastest.
Arguments:
- density: float32 [512, 512, 256], P('px', 'py'), may hold values from -6 to 6
- external: float32 [512, 512, 256], P('px', 'py'), may hold values from -6 to 6
- orbitals: float32 [64, 8, 24, 576], P(('px', 'py')), may hold values from -6 to 6
- anchors: int32 [64, 3], P(('px', 'py')), may hold values from 0 to 511, as said below
- weights: int32 [64], P(('px', 'py')), may hold values from -1 to 1, as said below
- degrees: int32 [64], P(('px', 'py')), may hold values from 4 to 24
Outputs:
- hartree_field: float32 [512, 512, 256], P('px', 'py')
- filtered: float32 [64, 8, 24, 576], P(('px', 'py'))
- new_density: float32 [512, 512, 256], P('px', 'py')
The draws below stay inside these ranges and needn't reach their ends.
Inputs may be any that keep to these rules, and one draw needn't show every extreme that they name: `anchors`: fragment f lies on device f // 2 of the joined px, py axes; its anchor's first two coordinates lie in that device's block of the grid, its third coordinate is at most 232. `weights`: each weight is -1 or +1.
All inputs are finite; a program needn't handle non-finite values.
Results may differ from the reference program's by a relative error of at most 0.0003.
Values sent between devices are 32-bit elements; how exact they have to be, the bound alone decides.
A program may use at most 128 MiB of HBM per device.

```python
import jax
import jax.numpy as jnp
from jax import lax

NX = 512
NY = 512
NZ = 256
FRAG = 24
NORB = 8
FRAG_DEV = 2
DEG_MIN = 4
DEG_MAX = 24
NFRAG = 64
N_PX = 8
N_PY = 4


def draw_anchors(key, part):
    block_rows = NX // N_PX
    block_cols = NY // N_PY
    device_ids = jnp.arange(NFRAG, dtype=jnp.int32) // FRAG_DEV
    key_x, key_y, key_z = jax.random.split(jax.random.fold_in(key, 11), 3)
    first = device_ids // N_PY * block_rows + jax.random.randint(key_x, (NFRAG,), 0, block_rows)
    second = device_ids % N_PY * block_cols + jax.random.randint(key_y, (NFRAG,), 0, block_cols)
    third = jax.random.randint(key_z, (NFRAG,), 0, NZ - FRAG + 1)
    return jnp.stack([first, second, third], 1).astype(jnp.int32)


def draw_weights(key, part):
    signs = jax.random.randint(jax.random.fold_in(key, 23), (NFRAG,), 0, 2)
    return (2 * signs - 1).astype(jnp.int32)


def place_ends(result, stream_key, low, largest):
    index_at = [jax.random.randint(jax.random.fold_in(stream_key, axis), (), 0, length) for axis, length in enumerate(result.shape)]
    longest = result.shape.index(max(result.shape))
    next_to = index_at[:longest] + [(index_at[longest] + 1) % result.shape[longest]] + index_at[longest + 1:]
    return result.at[tuple(index_at)].set(low).at[tuple(next_to)].set(largest)


def level_of(stream_key, dims, cuts, low, high):
    loudness = 1.0
    for position, shards_of in cuts:
        draws = jax.random.uniform(jax.random.fold_in(jax.random.fold_in(stream_key, 6), position), (shards_of,), jnp.float32, low / len(cuts), high / len(cuts))
        loudness = loudness * jnp.repeat(jnp.exp(draws), dims[position] // shards_of).reshape((-1,) + (1,) * (len(dims) - 1 - position))
    return loudness


def noise(stream_key, extent, scale, bound, cuts=(), kind=jnp.bfloat16):
    result = jax.random.normal(stream_key, extent, jnp.float32) * scale
    if len(cuts) > 0:
        result = level_of(stream_key, extent, cuts, -0.22, 0.18) * result
    return jnp.clip(result, min=-bound, max=bound).astype(kind)


def setup_inputs(seed: int = 0) -> dict:
    splits = jax.random.split(jax.random.key(seed), 7)
    density = noise(splits[0], (NX, NY, NZ), 1.0, 6.0, ((0, 8), (1, 4)), jnp.float32)
    external = noise(splits[1], (NX, NY, NZ), 1.0, 6.0, ((0, 8), (1, 4)), jnp.float32)
    orbitals = noise(splits[2], (NFRAG, NORB, FRAG, FRAG * FRAG), 1.0, 6.0, ((0, 32),), jnp.float32)
    anchors = draw_anchors(jax.random.fold_in(splits[6], 71), 0)
    weights = draw_weights(jax.random.fold_in(splits[6], 71), 0)
    degrees = place_ends(jax.random.randint(splits[5], (NFRAG,), DEG_MIN, DEG_MAX + 1), jax.random.fold_in(splits[5], 1), DEG_MIN, DEG_MAX).astype(jnp.int32)
    return dict(density=density, external=external, orbitals=orbitals, anchors=anchors, weights=weights, degrees=degrees)


screening = 0.002
window_gap = 0.1
kinetic_top = 6.0
highest = lax.Precision.HIGHEST

def sine_table(length):
    indices = jnp.arange(1, length + 1, dtype=jnp.int32)
    product = indices[:, None] * indices[None, :] % (2 * length + 2)
    angle = product.astype(jnp.float32) * (jnp.pi / (length + 1))
    return jnp.sin(angle) * jnp.sqrt(2.0 / (length + 1))

def eigen_values(start, count, length):
    wave = (start + jnp.arange(count, dtype=jnp.int32) + 1).astype(jnp.float32)
    return 2.0 - 2.0 * jnp.cos(wave * (jnp.pi / (length + 1)))

def along_first(field, table):
    return jnp.einsum('abc,ak->kbc', field, table, precision=highest)

def along_second(field, table):
    return jnp.einsum('abc,bk->akc', field, table, precision=highest)

def along_third(field, table):
    return jnp.einsum('abc,ck->abk', field, table, precision=highest)

def neighbours(field):
    frag_edge = field.shape[-2]
    zero_row = jnp.zeros_like(field[..., :1, :])
    total = jnp.concatenate([field[..., 1:, :], zero_row], -2) + jnp.concatenate([zero_row, field[..., :-1, :]], -2)
    zero_cols = jnp.zeros_like(field[..., :frag_edge])
    total = total + jnp.concatenate([field[..., frag_edge:], zero_cols], -1) + jnp.concatenate([zero_cols, field[..., :-frag_edge]], -1)
    zero_one = jnp.zeros_like(field[..., :1])
    inner = jnp.arange(field.shape[-1], dtype=jnp.int32) % frag_edge
    forward = jnp.concatenate([field[..., 1:], zero_one], -1)
    backward = jnp.concatenate([zero_one, field[..., :-1]], -1)
    total = total + jnp.where(inner == frag_edge - 1, 0.0, forward) + jnp.where(inner == 0, 0.0, backward)
    return total

def chebyshev(orbital_set, box, degree_set, steps):
    low = lax.optimization_barrier(jnp.min(box, axis=(1, 2))) + window_gap
    high = lax.optimization_barrier(jnp.max(box, axis=(1, 2))) + kinetic_top
    centre = (0.5 * (high + low))[:, None, None, None]
    half_width = (0.5 * (high - low))[:, None, None, None]
    potential = box[:, None]

    def advance(counter, state):
        before, current = state
        image = 3.0 * current - 0.5 * neighbours(current) + potential * current
        scaled = (image - centre * current) / half_width
        following = jnp.where(counter == 0, scaled, 2.0 * scaled - before)
        live = (counter < degree_set)[:, None, None, None]
        return (jnp.where(live, current, before), jnp.where(live, following, current))
    before, current = lax.fori_loop(0, steps, advance, (orbital_set, orbital_set))
    cells = orbital_set.shape[2] ** 3
    squares = lax.optimization_barrier(jnp.sum(current * current, axis=(2, 3), keepdims=True))
    return current * jnp.sqrt(cells / (squares + 1e-06))

def hartree(density):
    table_x = sine_table(NX)
    table_y = sine_table(NY)
    table_z = sine_table(NZ)
    spectrum = along_third(density, table_z)
    spectrum = along_second(spectrum, table_y)
    spectrum = along_first(spectrum, table_x)
    divisor = eigen_values(0, NX, NX)[:, None, None] + eigen_values(0, NY, NY)[None, :, None] + eigen_values(0, NZ, NZ)[None, None, :] + screening
    spectrum = along_first(spectrum / divisor, table_x)
    spectrum = along_second(spectrum, table_y)
    return along_third(spectrum, table_z)

def reference(density, external, orbitals, anchors, weights, degrees):
    hartree_field = hartree(density)
    potential = hartree_field + external
    padded = jnp.pad(potential, ((0, FRAG), (0, FRAG), (0, 0)))

    def filter_one(parcel):
        orbital_set, corner, degree = parcel
        box = lax.dynamic_slice(padded, (corner[0], corner[1], corner[2]), (FRAG, FRAG, FRAG))
        box = box.reshape(1, FRAG, FRAG * FRAG)
        return chebyshev(orbital_set[None], box, degree[None], DEG_MAX)[0]
    filtered = lax.map(filter_one, (orbitals, anchors, degrees))
    weight_scale = weights.astype(jnp.float32) / NORB
    contribution = weight_scale[:, None, None] * lax.optimization_barrier(jnp.sum(filtered * filtered, axis=1))

    def place(counter, total):
        corner = (anchors[counter, 0], anchors[counter, 1], anchors[counter, 2])
        block = contribution[counter].reshape(FRAG, FRAG, FRAG)
        current = lax.dynamic_slice(total, corner, (FRAG, FRAG, FRAG))
        return lax.dynamic_update_slice(total, current + block, corner)
    widened = jnp.zeros((NX + FRAG, NY + FRAG, NZ), jnp.float32)
    widened = lax.fori_loop(0, NFRAG, place, widened)
    return (hartree_field, filtered, widened[:NX, :NY])
```

```python
import functools

import jax
import jax.numpy as jnp
import ml_dtypes
import numpy as np
from jax import lax
from jax.experimental import pallas as pl
from jax.experimental.pallas import tpu as pltpu
from jax.sharding import PartitionSpec as P

screening = 0.002
window_gap = 0.1
kinetic_top = 6.0
highest = lax.Precision.HIGHEST
vmem_bytes = 56 * 1024 * 1024
f32 = jnp.float32
bf16 = jnp.bfloat16


def sine_table(length):
    index = np.arange(1, length + 1, dtype=np.int64)
    product = index[:, None] * index[None, :] % (2 * length + 2)
    return np.sin(np.pi * product / (length + 1)) * np.sqrt(2.0 / (length + 1))


def eigen_values(length):
    index = np.arange(1, length + 1, dtype=np.float64)
    return 4.0 * np.sin(np.pi * index / (2 * (length + 1))) ** 2


def decay(shift):
    return 2.0 * np.arcsinh(0.5 * np.sqrt(shift))


def halves(table):
    high = table.astype(np.float32).astype(ml_dtypes.bfloat16)
    low = (table - high.astype(np.float64)).astype(np.float32).astype(ml_dtypes.bfloat16)
    return high, low


def split(value):
    high = value.astype(bf16)
    return high, (value - high.astype(f32)).astype(bf16)


def dot(left, right):
    return jnp.dot(left, right, preferred_element_type=f32)


def third_product(value, high_ref, low_ref):
    high, low = split(value)
    return dot(high, high_ref[...]) + (dot(high, low_ref[...]) + dot(low, high_ref[...]))


def second_product(value, table_ref):
    rows = value.shape[0]
    both = dot(table_ref[...], jnp.concatenate(split(value), 0))
    return both[:rows] + both[rows:]


def rows_of(count):
    return min(32, count)


def forward_kernel(
    x_ref, zh_ref, zl_ref, sy_ref, r_ref, s0_ref, s1_ref, p_ref, w_ref, carry, left, right
):
    step = pl.program_id(0)
    slabs, cols, depth = x_ref.shape
    rows = p_ref.shape[0]

    @pl.when(step == 0)
    def _():
        carry[...] = jnp.zeros_like(carry)

    turned = third_product(x_ref[...].reshape(slabs * cols, depth), zh_ref, zl_ref)
    for slab in range(slabs):
        value = second_product(turned[slab * cols : (slab + 1) * cols], sy_ref)
        value = r_ref[...] * carry[...] + value
        carry[...] = value
        p_ref[step * slabs + slab] = value

    @pl.when(step == pl.num_programs(0) - 1)
    def _():
        left[...] = jnp.zeros_like(left)
        right[...] = jnp.zeros_like(right)
        part = rows_of(cols)
        for start in range(0, cols, part):
            span = pl.ds(start, part)
            ratio = r_ref[span, :]
            first = s0_ref[span, :]
            last = s1_ref[span, :]

            def back(count, u):
                row = rows - 1 - count
                u = ratio * (u + p_ref[row, span, :])
                left[row] += jnp.sum((first * u).reshape(part // 8, 8, depth), 0)
                right[row] += jnp.sum((last * u).reshape(part // 8, 8, depth), 0)
                return u

            u = lax.fori_loop(0, rows, back, jnp.zeros((part, depth), f32))
            w_ref[pl.ds(2 * rows + cols + start, part), :] = u
        w_ref[pl.ds(0, rows), :] = jnp.sum(left[...], 1)
        w_ref[pl.ds(rows, rows), :] = jnp.sum(right[...], 1)
        w_ref[pl.ds(2 * rows, cols), :] = carry[...]


def backward_kernel(
    p_ref, w_ref, zh_ref, zl_ref, sy_ref, r_ref, s0_ref, s1_ref, out_ref, q, carry, turned
):
    step = pl.program_id(0)
    steps = pl.num_programs(0)
    slabs, cols, depth = out_ref.shape
    rows = p_ref.shape[0]

    @pl.when(step == 0)
    def _():
        part = rows_of(cols)
        for start in range(0, cols, part):
            span = pl.ds(start, part)
            ratio = r_ref[span, :]
            first = s0_ref[span, :]
            last = s1_ref[span, :]

            def ahead(row, p):
                lower = w_ref[pl.ds(row, 1), :]
                upper = w_ref[pl.ds(rows + row, 1), :]
                p = ratio * p + (first * lower + last * upper)
                q[row, span, :] = p_ref[row, span, :] + p
                return p

            lax.fori_loop(0, rows, ahead, w_ref[pl.ds(2 * rows + start, part), :])
        carry[...] = w_ref[pl.ds(2 * rows + cols, cols), :]

    base = (steps - 1 - step) * slabs
    for slab in range(slabs - 1, -1, -1):
        u = r_ref[...] * (carry[...] + q[base + slab])
        carry[...] = u
        turned[slab] = second_product(u, sy_ref)
    value = third_product(turned[...].reshape(slabs * cols, depth), zh_ref, zl_ref)
    out_ref[...] = value.reshape(slabs, cols, depth)


def whole(shape):
    return pl.BlockSpec(shape, lambda step: (0,) * len(shape))


def params():
    return pltpu.CompilerParams(vmem_limit_bytes=vmem_bytes)


def hartree(density, peers_x, peers_y):
    rows, cols, depth = density.shape
    span_x = rows * peers_x
    devices = peers_x * peers_y
    chunk = -(-depth // devices)
    padded = chunk * devices
    slabs = min(8, rows)
    steps = rows // slabs
    z_high, z_low = halves(sine_table(depth))
    y_table = sine_table(cols)
    y_high, y_low = halves(y_table)
    y_both = np.block([[y_high, y_high], [y_low, y_low]])
    z_values = np.pad(eigen_values(depth), (0, padded - depth), mode="edge")
    block_shift = eigen_values(cols)[None, :] + z_values[:, None] + screening
    theta_all = decay(block_shift)
    ratio = np.exp(-theta_all[:depth].T).astype(np.float32)
    first = y_table[0].astype(np.float32)
    last = y_table[-1].astype(np.float32)
    first_wide = np.broadcast_to(first[:, None], (cols, depth)).copy()
    last_wide = np.broadcast_to(last[:, None], (cols, depth)).copy()
    edge_theta = decay(eigen_values(span_x)[None, :] + z_values[:, None] + screening)
    edge_near = np.exp(-edge_theta) * np.expm1(-2 * cols * edge_theta)
    edge_near = (edge_near / np.expm1(-2 * (cols + 1) * edge_theta)).astype(np.float32)
    edge_far = np.exp(-cols * edge_theta) * np.expm1(-2 * edge_theta)
    edge_far = (edge_far / np.expm1(-2 * (cols + 1) * edge_theta)).astype(np.float32)
    width = 2 * rows + 2 * cols
    tables = (z_high, z_low, y_both, ratio, first_wide, last_wide)
    table_specs = [whole(table.shape) for table in tables]

    p, edges = pl.pallas_call(
        forward_kernel,
        grid=(steps,),
        in_specs=[pl.BlockSpec((slabs, cols, depth), lambda step: (step, 0, 0))] + table_specs,
        out_specs=[whole((rows, cols, depth)), whole((width, depth))],
        out_shape=[
            jax.ShapeDtypeStruct((rows, cols, depth), f32),
            jax.ShapeDtypeStruct((width, depth), f32),
        ],
        scratch_shapes=[
            pltpu.VMEM((cols, depth), f32),
            pltpu.VMEM((rows, 8, depth), f32),
            pltpu.VMEM((rows, 8, depth), f32),
        ],
        compiler_params=params(),
        name="solve_ahead",
    )(density, *tables)

    owner = lax.axis_index("px") * peers_y + lax.axis_index("py")

    def owned(table):
        return lax.dynamic_slice_in_dim(jnp.asarray(table), owner * chunk, chunk, 0)

    theta = owned(theta_all.astype(np.float32))
    r = jnp.exp(-theta)
    gap = -jnp.expm1(-2.0 * theta)
    block_power = jnp.exp(-rows * theta)
    spread = r * r * -jnp.expm1(-2.0 * rows * theta) / gap
    closing = gap / -jnp.expm1(-2.0 * (span_x + 1) * theta)
    place = jnp.arange(rows, dtype=f32)[None, :, None]
    to_end = jnp.exp(-theta[:, None, :] * (rows - 1 - place))
    to_start = (
        jnp.exp(-theta[:, None, :] * (place + 1))
        * -jnp.expm1(-2.0 * theta[:, None, :] * (rows - place))
        / gap[:, None, :]
    )
    near = owned(edge_near)
    far = owned(edge_far)
    table_x = jnp.asarray(sine_table(span_x).astype(np.float32))

    def carries(ends, starts):
        entering = [jnp.zeros_like(ends[0])]
        for i in range(1, peers_x):
            entering.append(ends[i - 1] + block_power * entering[-1])

        def sweep(entering):
            values = [jnp.zeros_like(ends[0])]
            for i in range(peers_x - 1, -1, -1):
                values.append(starts[i] + spread * entering[i] + block_power * values[-1])
            return values[::-1]

        mirror = -closing * sweep(entering)[0]
        fixed = []
        for i in range(peers_x):
            fixed.append(entering[i] + mirror)
            mirror = block_power * mirror
        return jnp.stack(fixed), jnp.stack(sweep(fixed)[1:])

    sent = jnp.pad(edges.T, ((0, padded - depth), (0, 0))).reshape(devices, chunk, width)
    held = lax.all_to_all(sent, ("px", "py"), split_axis=0, concat_axis=0, tiled=True)
    held = held.reshape(peers_x, peers_y, chunk, width)
    ends = held[..., 2 * rows : 2 * rows + cols]
    starts = held[..., 2 * rows + cols :]
    entering, leaving = carries(ends, starts)
    sides = jnp.stack([jnp.asarray(first), jnp.asarray(last)])[:, None, None, None, :]
    edge_values = jnp.stack([held[..., :rows], held[..., rows : 2 * rows]])
    edge_values = (
        edge_values
        + jnp.einsum("sijck,cxk->sijcx", sides * (r * entering), to_start, precision=highest)
        + jnp.einsum("sijck,cxk->sijcx", sides * (r * leaving), to_end, precision=highest)
    )
    lines = edge_values.transpose(0, 2, 3, 1, 4).reshape(2, peers_y, chunk, span_x)
    lines = jnp.einsum("sjcx,xk->sjck", lines, table_x, precision=highest)
    known = jnp.zeros_like(near)
    slope = jnp.zeros_like(near)
    steps_back = []
    for j in range(peers_y):
        scale = 1.0 / (1.0 - near * slope)
        middle = (lines[0, j] + near * known) * scale
        steps_back.append((middle, far * scale, known, slope))
        known = lines[1, j] + far * (known + slope * middle)
        slope = near + far * slope * far * scale
    above = jnp.zeros_like(near)
    lower = []
    upper = []
    for j in range(peers_y - 1, -1, -1):
        middle, reach, known, slope = steps_back[j]
        upper.append(above)
        above = middle + reach * above
        lower.append(known + slope * above)
    outer = jnp.stack([jnp.stack(lower[::-1]), jnp.stack(upper[::-1])])
    outer = jnp.einsum("sjck,xk->sjcx", outer, table_x, precision=highest)
    outer = outer.reshape(2, peers_y, chunk, peers_x, rows).transpose(0, 3, 1, 2, 4)
    more_ends = jnp.sum(
        sides * jnp.einsum("sijcx,cxk->sijck", outer, to_end, precision=highest), 0
    )
    more_starts = jnp.sum(
        sides * jnp.einsum("sijcx,cxk->sijck", outer, to_start, precision=highest), 0
    )
    entering, leaving = carries(ends + more_ends, starts + more_starts)
    answer = jnp.concatenate([outer[0], outer[1], entering, leaving], -1)
    answer = answer.reshape(devices, chunk, width)
    answer = lax.all_to_all(answer, ("px", "py"), split_axis=0, concat_axis=0, tiled=True)
    answer = answer.reshape(padded, width)[:depth].T

    return pl.pallas_call(
        backward_kernel,
        grid=(steps,),
        in_specs=[whole((rows, cols, depth)), whole((width, depth))] + table_specs,
        out_specs=pl.BlockSpec((slabs, cols, depth), lambda step: (steps - 1 - step, 0, 0)),
        out_shape=jax.ShapeDtypeStruct((rows, cols, depth), f32),
        scratch_shapes=[
            pltpu.VMEM((rows, cols, depth), f32),
            pltpu.VMEM((cols, depth), f32),
            pltpu.VMEM((slabs, cols, depth), f32),
        ],
        compiler_params=params(),
        name="solve_back",
    )(p, answer, *tables)


def cut_kernel(edge, corner_ref, field_ref, other_ref, out_ref, held, sems):
    rows, cols, depth = field_ref.shape
    count, _, wide, tall, _ = held.shape

    def corner(index):
        return corner_ref[index, 0], corner_ref[index, 1], corner_ref[index, 2]

    def meets(index):
        x, y, _ = corner(index)
        return (x > -edge) & (x < rows) & (y > -edge) & (y < cols)

    def window(index):
        x, y, _ = corner(index)
        x_start = jnp.clip(x, 0, rows - wide)
        y_start = jnp.clip(jnp.maximum(y, 0) // 8 * 8, 0, cols - tall)
        return x_start, pl.multiple_of(y_start, 8)

    def copies(index):
        x_start, y_start = window(index)
        return [
            pltpu.make_async_copy(
                source.at[pl.ds(x_start, wide), pl.ds(y_start, tall), :],
                held.at[index, which],
                sems.at[index, which],
            )
            for which, source in enumerate((field_ref, other_ref))
        ]

    for index in range(count):

        @pl.when(meets(index))
        def _():
            for copy in copies(index):
                copy.start()

    for index in range(count):

        @pl.when(jnp.logical_not(meets(index)))
        def _():
            out_ref[index] = jnp.zeros(out_ref.shape[1:], f32)

        @pl.when(meets(index))
        def _():
            for copy in copies(index):
                copy.wait()
            x, y, z = corner(index)
            x_start, y_start = window(index)
            turn_y = lax.rem(y_start - y + tall, tall)
            turn_z = lax.rem(depth - z, depth)
            place = y + lax.broadcasted_iota(jnp.int32, (edge, edge), 0)
            inside = (place >= 0) & (place < cols)

            def one(k, _):
                row = jnp.clip(x + k, 0, rows - 1) - x_start
                value = held[index, 0, row] + held[index, 1, row]
                value = pltpu.roll(value, turn_y, 0)
                value = pltpu.roll(value, turn_z, 1)
                here = (x + k >= 0) & (x + k < rows)
                out_ref[index, k] = jnp.where(inside & here, value[:edge, :edge], 0.0)
                return 0

            lax.fori_loop(0, edge, one, 0)


def filter_kernel(
    degree_ref, weight_ref, box_ref, orbital_ref, out_ref, share_ref, state, slope_ref
):
    which = pl.program_id(0)
    _, orbitals, edge, merged = orbital_ref.shape
    lanes = state.shape[-1]
    box = box_ref[0]
    low = jnp.min(box) + window_gap
    high = jnp.max(box) + kinetic_top
    centre = 0.5 * (high + low)
    lane = lax.broadcasted_iota(jnp.int32, (orbitals, lanes), 1)
    inner = lax.rem(lane, edge)
    not_low = inner != 0
    not_high = inner != edge - 1
    inverse = 2.0 / (high - low + jnp.zeros((orbitals, lanes), f32))
    hop = jnp.where(lane < merged, -inverse, 0.0)
    state[...] = jnp.zeros_like(state)
    slope_ref[...] = jnp.zeros_like(slope_ref)
    state[0, 1 : edge + 1, :, :merged] = jnp.swapaxes(orbital_ref[0], 0, 1)
    for x in range(edge):
        row = (3.0 - centre + box[x : x + 1]) * (2.0 * inverse[:1, :merged])
        slope_ref[x, :, :merged] = jnp.broadcast_to(row, (orbitals, merged))

    def image(source, x, before, current, after):
        total = before + after
        total = total + pltpu.roll(current, edge, 1) + pltpu.roll(current, lanes - edge, 1)
        total = total + pltpu.roll(jnp.where(not_high, current, 0.0), 1, 1)
        total = total + pltpu.roll(jnp.where(not_low, current, 0.0), lanes - 1, 1)
        return slope_ref[x] * current + hop * total

    def advance(source, target, opening):
        before = state[source, 0]
        current = state[source, 1]
        for x in range(edge):
            after = state[source, x + 2]
            value = image(source, x, before, current, after)
            if opening:
                state[target, x + 1] = 0.5 * value
            else:
                state[target, x + 1] = value - state[target, x + 1]
            before, current = current, after

    degree = degree_ref[which]

    @pl.when(degree > 0)
    def _():
        advance(0, 1, True)

    def both(count, _):
        advance(1, 0, False)
        advance(0, 1, False)
        return 0

    lax.fori_loop(0, lax.div(degree - 1, 2), both, 0)
    even = lax.rem(degree, 2) == 0

    @pl.when(even & (degree > 0))
    def _():
        advance(1, 0, False)

    final = jnp.where(even, 0, 1)
    squares = jnp.zeros((orbitals, lanes), f32)
    for x in range(edge):
        value = state[final, x + 1]
        squares = squares + value * value
    total = jnp.sum(squares, axis=1, keepdims=True)
    scale = jnp.sqrt(edge**3 / (total + 1e-06))
    weight = weight_ref[which].astype(f32) / orbitals
    for x in range(edge):
        value = state[final, x + 1] * scale
        state[final, x + 1] = value
        share = weight * jnp.sum(value * value, axis=0, keepdims=True)
        share_ref[0, x : x + 1] = share[:, :merged]
    out_ref[0] = jnp.swapaxes(state[final, 1 : edge + 1], 0, 1)[:, :, :merged]


def patch_kernel(edge, margin, corner_ref, share_ref, out_ref, total, sem):
    rows, cols, depth = out_ref.shape
    count, _, tall, lanes = share_ref.shape

    def clear(row, _):
        total[row] = jnp.zeros(total.shape[1:], f32)
        return 0

    lax.fori_loop(0, rows, clear, 0)
    for index in range(count):
        x = corner_ref[index, 0]
        y = corner_ref[index, 1]
        z = corner_ref[index, 2]

        @pl.when((x > -edge) & (x < rows) & (y > -edge) & (y < cols))
        def _():
            start = (y + margin) // 8 * 8
            turn = y + margin - start
            span = pl.ds(pl.multiple_of(start, 8), tall)

            def one(k, _):
                value = share_ref[index, k]
                if depth > lanes:
                    value = jnp.concatenate([value, jnp.zeros((tall, depth - lanes), f32)], 1)
                value = pltpu.roll(value, turn, 0)
                value = pltpu.roll(value, z, 1)
                total[x + k, span, :] += value
                return 0

            lax.fori_loop(jnp.maximum(0, -x), jnp.minimum(edge, rows - x), one, 0)

    copy = pltpu.make_async_copy(total.at[:, pl.ds(margin, cols), :], out_ref, sem)
    copy.start()
    copy.wait()


def body(density, external, orbitals, anchors, weights, degrees):
    rows, cols, depth = density.shape
    count, orbital_count, edge, merged = orbitals.shape
    peers_x = lax.axis_size("px")
    peers_y = lax.axis_size("py")
    hops = [
        (a, b)
        for a in range((rows + edge - 2) // rows + 1)
        for b in range((cols + edge - 2) // cols + 1)
    ]

    def moved(value, a, b):
        if a == 0 and b == 0:
            return value
        pairs = [
            (i * peers_y + j, (i + a) * peers_y + j + b)
            for i in range(peers_x)
            for j in range(peers_y)
            if 0 <= i + a < peers_x and 0 <= j + b < peers_y
        ]
        return lax.ppermute(value, ("px", "py"), pairs)

    corners = jnp.concatenate([moved(anchors, a, b) for a, b in hops], 0)
    origin = jnp.stack([lax.axis_index("px") * rows, lax.axis_index("py") * cols, 0])
    corners = corners - origin[None, :].astype(jnp.int32)
    total = count * len(hops)

    field = hartree(density, peers_x, peers_y)

    scalars = pl.BlockSpec(memory_space=pltpu.SMEM)
    vectors = pl.BlockSpec(memory_space=pltpu.VMEM)
    anywhere = pl.BlockSpec(memory_space=pl.ANY)
    tall = -(-(edge + 7) // 8) * 8
    wide = min(edge, rows)
    pieces = pl.pallas_call(
        functools.partial(cut_kernel, edge),
        in_specs=[scalars, anywhere, anywhere],
        out_specs=vectors,
        out_shape=jax.ShapeDtypeStruct((total, edge, edge, edge), f32),
        scratch_shapes=[
            pltpu.VMEM((total, 2, wide, tall, depth), f32),
            pltpu.SemaphoreType.DMA((total, 2)),
        ],
        compiler_params=params(),
        name="cut_boxes",
    )(corners, field, external)
    pieces = pieces.reshape(len(hops), count, edge, merged)
    boxes = sum(moved(pieces[index], -a, -b) for index, (a, b) in enumerate(hops))

    lanes = -(-(merged + edge) // 128) * 128
    filtered, shares = pl.pallas_call(
        filter_kernel,
        grid=(count,),
        in_specs=[
            scalars,
            scalars,
            pl.BlockSpec((1, edge, merged), lambda f: (f, 0, 0)),
            pl.BlockSpec((1, orbital_count, edge, merged), lambda f: (f, 0, 0, 0)),
        ],
        out_specs=[
            pl.BlockSpec((1, orbital_count, edge, merged), lambda f: (f, 0, 0, 0)),
            pl.BlockSpec((1, edge, merged), lambda f: (f, 0, 0)),
        ],
        out_shape=[
            jax.ShapeDtypeStruct(orbitals.shape, f32),
            jax.ShapeDtypeStruct((count, edge, merged), f32),
        ],
        scratch_shapes=[
            pltpu.VMEM((2, edge + 2, orbital_count, lanes), f32),
            pltpu.VMEM((edge, orbital_count, lanes), f32),
        ],
        compiler_params=params(),
        name="filter_orbitals",
    )(degrees, weights, boxes, orbitals)

    parts = jnp.concatenate([moved(shares, a, b) for a, b in hops], 0)
    parts = parts.reshape(total, edge, edge, edge)
    side = min(128, depth)
    parts = jnp.pad(parts, ((0, 0), (0, 0), (0, tall - edge), (0, side - edge)))
    margin = tall
    new_density = pl.pallas_call(
        functools.partial(patch_kernel, edge, margin),
        in_specs=[scalars, vectors],
        out_specs=anywhere,
        out_shape=jax.ShapeDtypeStruct(density.shape, f32),
        scratch_shapes=[
            pltpu.VMEM((rows, cols + 2 * margin, depth), f32),
            pltpu.SemaphoreType.DMA,
        ],
        compiler_params=params(),
        name="patch_density",
    )(corners, parts)
    return (field, filtered, new_density)


def solution(mesh):
    placed = (
        P("px", "py", None),
        P("px", "py", None),
        P(("px", "py"), None, None, None),
        P(("px", "py"), None),
        P(("px", "py")),
        P(("px", "py")),
    )
    return jax.shard_map(
        body,
        mesh=mesh,
        in_specs=placed,
        out_specs=(P("px", "py", None), P(("px", "py"), None, None, None), P("px", "py", None)),
        check_vma=False,
    )
```

```python
import functools

import jax
import jax.numpy as jnp
import ml_dtypes
import numpy as np
from jax import lax
from jax.experimental import pallas as pl
from jax.experimental.pallas import tpu as pltpu
from jax.sharding import PartitionSpec as P

screening = 0.002
window_gap = 0.1
kinetic_top = 6.0
highest = lax.Precision.HIGHEST
vmem_bytes = 56 * 1024 * 1024
f32 = jnp.float32
bf16 = jnp.bfloat16


def sine_table(length):
    index = np.arange(1, length + 1, dtype=np.int64)
    product = index[:, None] * index[None, :] % (2 * length + 2)
    return np.sin(np.pi * product / (length + 1)) * np.sqrt(2.0 / (length + 1))


def eigen_values(length):
    index = np.arange(1, length + 1, dtype=np.float64)
    return 4.0 * np.sin(np.pi * index / (2 * (length + 1))) ** 2


def decay(shift):
    return 2.0 * np.arcsinh(0.5 * np.sqrt(shift))


def halves(table):
    high = table.astype(np.float32).astype(ml_dtypes.bfloat16)
    low = (table - high.astype(np.float64)).astype(np.float32).astype(ml_dtypes.bfloat16)
    return high, low


def split(value):
    high = value.astype(bf16)
    return high, (value - high.astype(f32)).astype(bf16)


def dot(left, right):
    return jnp.dot(left, right, preferred_element_type=f32)


def third_product(value, high_ref, low_ref):
    high, low = split(value)
    return dot(high, high_ref[...]) + (dot(high, low_ref[...]) + dot(low, high_ref[...]))


def second_product(value, table_ref):
    rows = value.shape[0]
    both = dot(table_ref[...], jnp.concatenate(split(value), 0))
    return both[:rows] + both[rows:]


def rows_of(count):
    return min(32, count)


def forward_kernel(
    x_ref, zh_ref, zl_ref, sy_ref, r_ref, s0_ref, s1_ref, p_ref, w_ref, carry, left, right
):
    step = pl.program_id(0)
    slabs, cols, depth = x_ref.shape
    rows = p_ref.shape[0]

    @pl.when(step == 0)
    def _():
        carry[...] = jnp.zeros_like(carry)

    turned = third_product(x_ref[...].reshape(slabs * cols, depth), zh_ref, zl_ref)
    for slab in range(slabs):
        value = second_product(turned[slab * cols : (slab + 1) * cols], sy_ref)
        value = r_ref[...] * carry[...] + value
        carry[...] = value
        p_ref[step * slabs + slab] = value

    @pl.when(step == pl.num_programs(0) - 1)
    def _():
        left[...] = jnp.zeros_like(left)
        right[...] = jnp.zeros_like(right)
        part = rows_of(cols)
        for start in range(0, cols, part):
            span = pl.ds(start, part)
            ratio = r_ref[span, :]
            first = s0_ref[span, :]
            last = s1_ref[span, :]

            def back(count, u):
                row = rows - 1 - count
                u = ratio * (u + p_ref[row, span, :])
                left[row] += jnp.sum((first * u).reshape(part // 8, 8, depth), 0)
                right[row] += jnp.sum((last * u).reshape(part // 8, 8, depth), 0)
                return u

            u = lax.fori_loop(0, rows, back, jnp.zeros((part, depth), f32), unroll=8)
            w_ref[pl.ds(2 * rows + cols + start, part), :] = u
        w_ref[pl.ds(0, rows), :] = jnp.sum(left[...], 1)
        w_ref[pl.ds(rows, rows), :] = jnp.sum(right[...], 1)
        w_ref[pl.ds(2 * rows, cols), :] = carry[...]


def backward_kernel(
    p_ref, w_ref, zh_ref, zl_ref, sy_ref, r_ref, s0_ref, s1_ref, out_ref, q, carry, turned
):
    step = pl.program_id(0)
    steps = pl.num_programs(0)
    slabs, cols, depth = out_ref.shape
    rows = p_ref.shape[0]

    @pl.when(step == 0)
    def _():
        part = rows_of(cols)
        for start in range(0, cols, part):
            span = pl.ds(start, part)
            ratio = r_ref[span, :]
            first = s0_ref[span, :]
            last = s1_ref[span, :]

            def ahead(row, p):
                lower = w_ref[pl.ds(row, 1), :]
                upper = w_ref[pl.ds(rows + row, 1), :]
                p = ratio * p + (first * lower + last * upper)
                q[row, span, :] = p_ref[row, span, :] + p
                return p

            opening = w_ref[pl.ds(2 * rows + start, part), :]
            lax.fori_loop(0, rows, ahead, opening, unroll=8)
        carry[...] = w_ref[pl.ds(2 * rows + cols, cols), :]

    base = (steps - 1 - step) * slabs
    for slab in range(slabs - 1, -1, -1):
        u = r_ref[...] * (carry[...] + q[base + slab])
        carry[...] = u
        turned[slab] = second_product(u, sy_ref)
    value = third_product(turned[...].reshape(slabs * cols, depth), zh_ref, zl_ref)
    out_ref[...] = value.reshape(slabs, cols, depth)


def whole(shape):
    return pl.BlockSpec(shape, lambda step: (0,) * len(shape))


def params():
    return pltpu.CompilerParams(vmem_limit_bytes=vmem_bytes)


def hartree(density, peers_x, peers_y):
    rows, cols, depth = density.shape
    span_x = rows * peers_x
    devices = peers_x * peers_y
    chunk = -(-depth // devices)
    padded = chunk * devices
    slabs = min(8, rows)
    steps = rows // slabs
    z_high, z_low = halves(sine_table(depth))
    y_table = sine_table(cols)
    y_high, y_low = halves(y_table)
    y_both = np.block([[y_high, y_high], [y_low, y_low]])
    z_values = np.pad(eigen_values(depth), (0, padded - depth), mode="edge")
    block_shift = eigen_values(cols)[None, :] + z_values[:, None] + screening
    theta_all = decay(block_shift)
    ratio = np.exp(-theta_all[:depth].T).astype(np.float32)
    first = y_table[0].astype(np.float32)
    last = y_table[-1].astype(np.float32)
    first_wide = np.broadcast_to(first[:, None], (cols, depth)).copy()
    last_wide = np.broadcast_to(last[:, None], (cols, depth)).copy()
    edge_theta = decay(eigen_values(span_x)[None, :] + z_values[:, None] + screening)
    edge_near = np.exp(-edge_theta) * np.expm1(-2 * cols * edge_theta)
    edge_near = (edge_near / np.expm1(-2 * (cols + 1) * edge_theta)).astype(np.float32)
    edge_far = np.exp(-cols * edge_theta) * np.expm1(-2 * edge_theta)
    edge_far = (edge_far / np.expm1(-2 * (cols + 1) * edge_theta)).astype(np.float32)
    width = 2 * rows + 2 * cols
    tables = (z_high, z_low, y_both, ratio, first_wide, last_wide)
    table_specs = [whole(table.shape) for table in tables]

    p, edges = pl.pallas_call(
        forward_kernel,
        grid=(steps,),
        in_specs=[pl.BlockSpec((slabs, cols, depth), lambda step: (step, 0, 0))] + table_specs,
        out_specs=[whole((rows, cols, depth)), whole((width, depth))],
        out_shape=[
            jax.ShapeDtypeStruct((rows, cols, depth), f32),
            jax.ShapeDtypeStruct((width, depth), f32),
        ],
        scratch_shapes=[
            pltpu.VMEM((cols, depth), f32),
            pltpu.VMEM((rows, 8, depth), f32),
            pltpu.VMEM((rows, 8, depth), f32),
        ],
        compiler_params=params(),
        name="solve_ahead",
    )(density, *tables)

    owner = lax.axis_index("px") * peers_y + lax.axis_index("py")

    def owned(table):
        return lax.dynamic_slice_in_dim(jnp.asarray(table), owner * chunk, chunk, 0)

    theta = owned(theta_all.astype(np.float32))
    r = jnp.exp(-theta)
    gap = -jnp.expm1(-2.0 * theta)
    block_power = jnp.exp(-rows * theta)
    spread = r * r * -jnp.expm1(-2.0 * rows * theta) / gap
    closing = gap / -jnp.expm1(-2.0 * (span_x + 1) * theta)
    place = jnp.arange(rows, dtype=f32)[None, :, None]
    to_end = jnp.exp(-theta[:, None, :] * (rows - 1 - place))
    to_start = (
        jnp.exp(-theta[:, None, :] * (place + 1))
        * -jnp.expm1(-2.0 * theta[:, None, :] * (rows - place))
        / gap[:, None, :]
    )
    near = owned(edge_near)
    far = owned(edge_far)
    table_x = jnp.asarray(sine_table(span_x).astype(np.float32))

    def carries(ends, starts):
        entering = [jnp.zeros_like(ends[0])]
        for i in range(1, peers_x):
            entering.append(ends[i - 1] + block_power * entering[-1])

        def sweep(entering):
            values = [jnp.zeros_like(ends[0])]
            for i in range(peers_x - 1, -1, -1):
                values.append(starts[i] + spread * entering[i] + block_power * values[-1])
            return values[::-1]

        mirror = -closing * sweep(entering)[0]
        fixed = []
        for i in range(peers_x):
            fixed.append(entering[i] + mirror)
            mirror = block_power * mirror
        return jnp.stack(fixed), jnp.stack(sweep(fixed)[1:])

    sent = jnp.pad(edges.T, ((0, padded - depth), (0, 0))).reshape(devices, chunk, width)
    held = lax.all_to_all(sent, ("px", "py"), split_axis=0, concat_axis=0, tiled=True)
    held = held.reshape(peers_x, peers_y, chunk, width)
    ends = held[..., 2 * rows : 2 * rows + cols]
    starts = held[..., 2 * rows + cols :]
    entering, leaving = carries(ends, starts)
    sides = jnp.stack([jnp.asarray(first), jnp.asarray(last)])[:, None, None, None, :]
    edge_values = jnp.stack([held[..., :rows], held[..., rows : 2 * rows]])
    edge_values = (
        edge_values
        + jnp.einsum("sijck,cxk->sijcx", sides * (r * entering), to_start, precision=highest)
        + jnp.einsum("sijck,cxk->sijcx", sides * (r * leaving), to_end, precision=highest)
    )
    lines = edge_values.transpose(0, 2, 3, 1, 4).reshape(2, peers_y, chunk, span_x)
    lines = jnp.einsum("sjcx,xk->sjck", lines, table_x, precision=highest)
    known = jnp.zeros_like(near)
    slope = jnp.zeros_like(near)
    steps_back = []
    for j in range(peers_y):
        scale = 1.0 / (1.0 - near * slope)
        middle = (lines[0, j] + near * known) * scale
        steps_back.append((middle, far * scale, known, slope))
        known = lines[1, j] + far * (known + slope * middle)
        slope = near + far * slope * far * scale
    above = jnp.zeros_like(near)
    lower = []
    upper = []
    for j in range(peers_y - 1, -1, -1):
        middle, reach, known, slope = steps_back[j]
        upper.append(above)
        above = middle + reach * above
        lower.append(known + slope * above)
    outer = jnp.stack([jnp.stack(lower[::-1]), jnp.stack(upper[::-1])])
    outer = jnp.einsum("sjck,xk->sjcx", outer, table_x, precision=highest)
    outer = outer.reshape(2, peers_y, chunk, peers_x, rows).transpose(0, 3, 1, 2, 4)
    more_ends = jnp.sum(
        sides * jnp.einsum("sijcx,cxk->sijck", outer, to_end, precision=highest), 0
    )
    more_starts = jnp.sum(
        sides * jnp.einsum("sijcx,cxk->sijck", outer, to_start, precision=highest), 0
    )
    entering, leaving = carries(ends + more_ends, starts + more_starts)
    answer = jnp.concatenate([outer[0], outer[1], entering, leaving], -1)
    answer = answer.reshape(devices, chunk, width)
    answer = lax.all_to_all(answer, ("px", "py"), split_axis=0, concat_axis=0, tiled=True)
    answer = answer.reshape(padded, width)[:depth].T

    return pl.pallas_call(
        backward_kernel,
        grid=(steps,),
        in_specs=[whole((rows, cols, depth)), whole((width, depth))] + table_specs,
        out_specs=pl.BlockSpec((slabs, cols, depth), lambda step: (steps - 1 - step, 0, 0)),
        out_shape=jax.ShapeDtypeStruct((rows, cols, depth), f32),
        scratch_shapes=[
            pltpu.VMEM((rows, cols, depth), f32),
            pltpu.VMEM((cols, depth), f32),
            pltpu.VMEM((slabs, cols, depth), f32),
        ],
        compiler_params=params(),
        name="solve_back",
    )(p, answer, *tables)


def cut_kernel(edge, corner_ref, field_ref, other_ref, out_ref, held, sems):
    rows, cols, depth = field_ref.shape
    count, _, wide, tall, _ = held.shape

    def corner(index):
        return corner_ref[index, 0], corner_ref[index, 1], corner_ref[index, 2]

    def meets(index):
        x, y, _ = corner(index)
        return (x > -edge) & (x < rows) & (y > -edge) & (y < cols)

    def window(index):
        x, y, _ = corner(index)
        x_start = jnp.clip(x, 0, rows - wide)
        y_start = jnp.clip(jnp.maximum(y, 0) // 8 * 8, 0, cols - tall)
        return x_start, pl.multiple_of(y_start, 8)

    def copies(index):
        x_start, y_start = window(index)
        return [
            pltpu.make_async_copy(
                source.at[pl.ds(x_start, wide), pl.ds(y_start, tall), :],
                held.at[index, which],
                sems.at[index, which],
            )
            for which, source in enumerate((field_ref, other_ref))
        ]

    for index in range(count):

        @pl.when(meets(index))
        def _():
            for copy in copies(index):
                copy.start()

    for index in range(count):

        @pl.when(jnp.logical_not(meets(index)))
        def _():
            out_ref[index] = jnp.zeros(out_ref.shape[1:], f32)

        @pl.when(meets(index))
        def _():
            for copy in copies(index):
                copy.wait()
            x, y, z = corner(index)
            x_start, y_start = window(index)
            turn_y = lax.rem(y_start - y + tall, tall)
            turn_z = lax.rem(depth - z, depth)
            place = y + lax.broadcasted_iota(jnp.int32, (edge, edge), 0)
            inside = (place >= 0) & (place < cols)

            def one(k, _):
                row = jnp.clip(x + k, 0, rows - 1) - x_start
                value = held[index, 0, row] + held[index, 1, row]
                value = pltpu.roll(value, turn_y, 0)
                value = pltpu.roll(value, turn_z, 1)
                here = (x + k >= 0) & (x + k < rows)
                out_ref[index, k] = jnp.where(inside & here, value[:edge, :edge], 0.0)
                return 0

            lax.fori_loop(0, edge, one, 0, unroll=8)


def to_blocks(value, edge, blocks):
    lane = lax.broadcasted_iota(jnp.int32, (value.shape[0], 128), 1)
    result = []
    for block in range(blocks):
        total = jnp.zeros((value.shape[0], 128), f32)
        for group in range(128 // edge):
            line = group * blocks + block
            if line >= edge:
                continue
            source, offset = divmod(line * edge, 128)
            target = group * edge
            first = min(edge, 128 - offset)
            for part, low, high in ((0, 0, first), (1, first, edge)):
                if low < high:
                    tile = value[:, (source + part) * 128 : (source + part + 1) * 128]
                    tile = pltpu.roll(tile, (target - offset) % 128, 1)
                    total = jnp.where((lane >= target + low) & (lane < target + high), tile, total)
        result.append(total)
    return result


def from_blocks(values, edge, tiles):
    blocks = len(values)
    lane = lax.broadcasted_iota(jnp.int32, values[0].shape, 1)
    result = []
    for tile in range(tiles):
        total = jnp.zeros(values[0].shape, f32)
        for line in range(edge):
            start = line * edge - tile * 128
            if start >= 128 or start + edge <= 0:
                continue
            group, block = divmod(line, blocks)
            moved = pltpu.roll(values[block], (start - group * edge) % 128, 1)
            total = jnp.where((lane >= start) & (lane < start + edge), moved, total)
        result.append(total)
    return jnp.concatenate(result, 1)


def filter_kernel(
    degree_ref, weight_ref, box_ref, orbital_ref, out_ref, share_ref, state, slope_ref, flat
):
    which = pl.program_id(0)
    _, orbitals, edge, merged = orbital_ref.shape
    blocks = state.shape[2]
    tiles = flat.shape[-1] // 128
    box = box_ref[0]
    low = jnp.min(box) + window_gap
    high = jnp.max(box) + kinetic_top
    centre = 0.5 * (high + low)
    lane = lax.broadcasted_iota(jnp.int32, (orbitals, 128), 1)
    inner = lax.rem(lane, edge)
    line = lax.div(lane, edge) * blocks
    not_low = inner != 0
    not_high = inner != edge - 1
    used = lane < 128 // edge * edge
    not_first = lane >= edge
    not_last = lane < (128 // edge - 1) * edge
    inverse = 2.0 / (high - low + jnp.zeros((orbitals, 128), f32))
    hop = [jnp.where(used & (line + block < edge), -inverse, 0.0) for block in range(blocks)]
    state[...] = jnp.zeros_like(state)
    flat[...] = jnp.zeros_like(flat)
    factor = 2.0 * inverse[:1, :1]
    for x in range(edge):
        row = (3.0 - centre + box[x : x + 1]) * factor
        flat[x, :, :merged] = jnp.broadcast_to(row, (orbitals, merged))

    def place_slope(x, _):
        for block, value in enumerate(to_blocks(flat[x], edge, blocks)):
            slope_ref[x, block] = value
        return 0

    lax.fori_loop(0, edge, place_slope, 0, unroll=4)
    flat[:, :, :merged] = jnp.swapaxes(orbital_ref[0], 0, 1)

    def place_state(x, _):
        for block, value in enumerate(to_blocks(flat[x], edge, blocks)):
            state[0, x + 1, block] = value
        return 0

    lax.fori_loop(0, edge, place_state, 0, unroll=4)

    def advance(source, target, opening):
        before = [state[source, 0, block] for block in range(blocks)]
        current = [state[source, 1, block] for block in range(blocks)]
        for x in range(edge):
            after = [state[source, x + 2, block] for block in range(blocks)]
            wrapped_up = pltpu.roll(jnp.where(not_first, current[0], 0.0), 128 - edge, 1)
            wrapped_down = pltpu.roll(jnp.where(not_last, current[-1], 0.0), edge, 1)
            for block in range(blocks):
                here = current[block]
                up = current[block + 1] if block + 1 < blocks else wrapped_up
                down = current[block - 1] if block > 0 else wrapped_down
                total = (before[block] + after[block]) + (up + down)
                total = total + (
                    pltpu.roll(jnp.where(not_high, here, 0.0), 1, 1)
                    + pltpu.roll(jnp.where(not_low, here, 0.0), 127, 1)
                )
                value = slope_ref[x, block] * here + hop[block] * total
                if opening:
                    state[target, x + 1, block] = 0.5 * value
                else:
                    state[target, x + 1, block] = value - state[target, x + 1, block]
            before, current = current, after

    degree = degree_ref[which]

    @pl.when(degree > 0)
    def _():
        advance(0, 1, True)

    def both(count, _):
        advance(1, 0, False)
        advance(0, 1, False)
        return 0

    lax.fori_loop(0, lax.div(degree - 1, 2), both, 0)
    even = lax.rem(degree, 2) == 0

    @pl.when(even & (degree > 0))
    def _():
        advance(1, 0, False)

    final = jnp.where(even, 0, 1)
    squares = jnp.zeros((orbitals, 128), f32)
    for x in range(edge):
        for block in range(blocks):
            value = state[final, x + 1, block]
            squares = squares + value * value
    total = jnp.sum(squares, axis=1, keepdims=True)
    scale = jnp.sqrt(edge**3 / (total + 1e-06))
    weight = weight_ref[which].astype(f32) / orbitals

    def finish(x, _):
        values = [state[final, x + 1, block] * scale for block in range(blocks)]
        value = from_blocks(values, edge, tiles)
        flat[x] = value
        share = weight * jnp.sum(value * value, axis=0, keepdims=True)
        share_ref[0, pl.ds(x, 1), :] = share[:, :merged]
        return 0

    lax.fori_loop(0, edge, finish, 0, unroll=4)
    out_ref[0] = jnp.swapaxes(flat[...], 0, 1)[:, :, :merged]


def exchange_kernel(hops, peers, sign, in_ref, out_ref, slots, send_sems, recv_sems):
    i = lax.axis_index("px")
    j = lax.axis_index("py")

    def exists(a, b):
        return (i + a >= 0) & (i + a < peers[0]) & (j + b >= 0) & (j + b < peers[1])

    barrier = pltpu.get_barrier_semaphore()
    both_ways = [(a * s, b * s) for a, b in hops[1:] for s in (1, -1)]
    for a, b in both_ways:

        @pl.when(exists(a, b))
        def _(a=a, b=b):
            pl.semaphore_signal(
                barrier, inc=1, device_id=(i + a, j + b), device_id_type=pl.DeviceIdType.MESH
            )

    pl.semaphore_wait(barrier, sum(exists(a, b).astype(jnp.int32) for a, b in both_ways))

    def copy(index):
        a, b = hops[index]
        return pltpu.make_async_remote_copy(
            src_ref=in_ref.at[index] if sign < 0 else in_ref,
            dst_ref=slots.at[index - 1],
            send_sem=send_sems.at[index - 1],
            recv_sem=recv_sems.at[index - 1],
            device_id=(i + sign * a, j + sign * b),
            device_id_type=pl.DeviceIdType.MESH,
        )

    for index in range(1, len(hops)):

        @pl.when(exists(sign * hops[index][0], sign * hops[index][1]))
        def _(index=index):
            copy(index).start()

    if sign < 0:
        out_ref[...] = in_ref[0]
    else:
        out_ref[0] = in_ref[...]
    for index in range(1, len(hops)):
        comes = exists(-sign * hops[index][0], -sign * hops[index][1])

        @pl.when(comes)
        def _(index=index):
            copy(index).wait_recv()
            if sign < 0:
                out_ref[...] += slots[index - 1]
            else:
                out_ref[index] = slots[index - 1]

        if sign > 0:

            @pl.when(jnp.logical_not(comes))
            def _(index=index):
                out_ref[index] = jnp.zeros(out_ref.shape[1:], f32)

    for index in range(1, len(hops)):

        @pl.when(exists(sign * hops[index][0], sign * hops[index][1]))
        def _(index=index):
            copy(index).wait_send()


def exchange(value, hops, peers, sign):
    shape = value.shape[1:] if sign < 0 else value.shape
    others = max(1, len(hops) - 1)
    out_shape = shape if sign < 0 else (len(hops),) + shape
    return pl.pallas_call(
        functools.partial(exchange_kernel, hops, peers, sign),
        in_specs=[pl.BlockSpec(memory_space=pltpu.VMEM)],
        out_specs=pl.BlockSpec(memory_space=pltpu.VMEM),
        out_shape=jax.ShapeDtypeStruct(out_shape, f32),
        scratch_shapes=[
            pltpu.VMEM((others,) + shape, f32),
            pltpu.SemaphoreType.DMA((others,)),
            pltpu.SemaphoreType.DMA((others,)),
        ],
        compiler_params=pltpu.CompilerParams(
            vmem_limit_bytes=vmem_bytes, has_side_effects=True, collective_id=0 if sign < 0 else 1
        ),
        name="gather_boxes" if sign < 0 else "spread_shares",
    )(value)


def patch_kernel(edge, margin, corner_ref, share_ref, out_ref, total, sem):
    rows, cols, depth = out_ref.shape
    count, _, tall, lanes = share_ref.shape

    def clear(row, _):
        total[edge + row, margin : margin + cols] = jnp.zeros((cols, depth), f32)
        return 0

    lax.fori_loop(0, rows, clear, 0)
    for index in range(count):
        x = corner_ref[index, 0]
        y = corner_ref[index, 1]
        z = corner_ref[index, 2]

        @pl.when((x > -edge) & (x < rows) & (y > -edge) & (y < cols))
        def _():
            start = (y + margin) // 8 * 8
            turn = y + margin - start
            span = pl.ds(pl.multiple_of(start, 8), tall)

            def one(k, _):
                value = share_ref[index, k]
                if depth > lanes:
                    value = jnp.concatenate([value, jnp.zeros((tall, depth - lanes), f32)], 1)
                value = pltpu.roll(value, turn, 0)
                value = pltpu.roll(value, z, 1)
                total[edge + x + k, span, :] += value
                return 0

            lax.fori_loop(0, edge, one, 0, unroll=8)

    copy = pltpu.make_async_copy(total.at[pl.ds(edge, rows), pl.ds(margin, cols), :], out_ref, sem)
    copy.start()
    copy.wait()


def body(density, external, orbitals, anchors, weights, degrees):
    rows, cols, depth = density.shape
    count, orbital_count, edge, merged = orbitals.shape
    peers_x = lax.axis_size("px")
    peers_y = lax.axis_size("py")
    hops = [
        (a, b)
        for a in range((rows + edge - 2) // rows + 1)
        for b in range((cols + edge - 2) // cols + 1)
    ]

    def moved(value, a, b):
        if a == 0 and b == 0:
            return value
        pairs = [
            (i * peers_y + j, (i + a) * peers_y + j + b)
            for i in range(peers_x)
            for j in range(peers_y)
            if 0 <= i + a < peers_x and 0 <= j + b < peers_y
        ]
        return lax.ppermute(value, ("px", "py"), pairs)

    corners = jnp.concatenate([moved(anchors, a, b) for a, b in hops], 0)
    origin = jnp.stack([lax.axis_index("px") * rows, lax.axis_index("py") * cols, 0])
    corners = corners - origin[None, :].astype(jnp.int32)
    total = count * len(hops)

    field = hartree(density, peers_x, peers_y)

    scalars = pl.BlockSpec(memory_space=pltpu.SMEM)
    vectors = pl.BlockSpec(memory_space=pltpu.VMEM)
    anywhere = pl.BlockSpec(memory_space=pl.ANY)
    tall = -(-(edge + 7) // 8) * 8
    wide = min(edge, rows)
    pieces = pl.pallas_call(
        functools.partial(cut_kernel, edge),
        in_specs=[scalars, anywhere, anywhere],
        out_specs=vectors,
        out_shape=jax.ShapeDtypeStruct((total, edge, edge, edge), f32),
        scratch_shapes=[
            pltpu.VMEM((total, 2, wide, tall, depth), f32),
            pltpu.SemaphoreType.DMA((total, 2)),
        ],
        compiler_params=params(),
        name="cut_boxes",
    )(corners, field, external)
    pieces = pieces.reshape(len(hops), count, edge, merged)
    boxes = exchange(pieces, hops, (peers_x, peers_y), -1)

    lanes = -(-merged // 128) * 128
    blocks = -(-edge // (128 // edge))
    filtered, shares = pl.pallas_call(
        filter_kernel,
        grid=(count,),
        in_specs=[
            scalars,
            scalars,
            pl.BlockSpec((1, edge, merged), lambda f: (f, 0, 0)),
            pl.BlockSpec((1, orbital_count, edge, merged), lambda f: (f, 0, 0, 0)),
        ],
        out_specs=[
            pl.BlockSpec((1, orbital_count, edge, merged), lambda f: (f, 0, 0, 0)),
            pl.BlockSpec((1, edge, merged), lambda f: (f, 0, 0)),
        ],
        out_shape=[
            jax.ShapeDtypeStruct(orbitals.shape, f32),
            jax.ShapeDtypeStruct((count, edge, merged), f32),
        ],
        scratch_shapes=[
            pltpu.VMEM((2, edge + 2, blocks, orbital_count, 128), f32),
            pltpu.VMEM((edge, blocks, orbital_count, 128), f32),
            pltpu.VMEM((edge, orbital_count, lanes), f32),
        ],
        compiler_params=params(),
        name="filter_orbitals",
    )(degrees, weights, boxes, orbitals)

    parts = exchange(shares, hops, (peers_x, peers_y), 1)
    parts = parts.reshape(total, edge, edge, edge)
    side = min(128, depth)
    parts = jnp.pad(parts, ((0, 0), (0, 0), (0, tall - edge), (0, side - edge)))
    margin = tall
    new_density = pl.pallas_call(
        functools.partial(patch_kernel, edge, margin),
        in_specs=[scalars, vectors],
        out_specs=anywhere,
        out_shape=jax.ShapeDtypeStruct(density.shape, f32),
        scratch_shapes=[
            pltpu.VMEM((rows + 2 * edge, cols + 2 * margin, depth), f32),
            pltpu.SemaphoreType.DMA,
        ],
        compiler_params=params(),
        name="patch_density",
    )(corners, parts)
    return (field, filtered, new_density)


def solution(mesh):
    placed = (
        P("px", "py", None),
        P("px", "py", None),
        P(("px", "py"), None, None, None),
        P(("px", "py"), None),
        P(("px", "py")),
        P(("px", "py")),
    )
    return jax.shard_map(
        body,
        mesh=mesh,
        in_specs=placed,
        out_specs=(P("px", "py", None), P(("px", "py"), None, None, None), P("px", "py", None)),
        check_vma=False,
    )
```
